32 devices in a mesh: layer: 8 (over y, x, core), rows: 4 (over z).
Axes of the slice: x: 2, y: 2, z: 4, core: 2. Of those that a mesh axis runs over, the one named last changes fastest.
Arguments:
- weights: bfloat16 [64, 32, 288], P('layer'), may hold values from -0.375 to 0.375
- image: float32 [3, 32, 64, 128], P(None, None, 'rows'), may hold values from -6 to 6
- guess: float32 [16, 3, 32, 64, 128], P('layer', None, None, 'rows'), may hold values from -6 to 6
Outputs:
- corrected: float32 [16, 3, 32, 64, 128], P('layer', None, None, 'rows')
The draws below stay inside these ranges and needn't reach their ends.
All inputs are finite; a program needn't handle non-finite values.
Results may differ from the reference program's by a relative error of at most 0.009.
Values may be sent and summed in bfloat16 or wider, within the bound.
A program may use at most 64 MiB of HBM per device.

```python
import jax
import jax.numpy as jnp
from jax import lax

C = 32
M = 4
L_DEV = 8
B = 3
IMG_W = 128
NL = 64
K = 16
IMG_ROWS = 64
N_LAYER = 8


def block_scale(own_key, shape, cuts, least, largest):
    loudness, own = 1.0, jax.random.fold_in(own_key, 6)
    for position, parts in cuts:
        steps = jnp.exp(jax.random.uniform(jax.random.fold_in(own, position), (parts,), jnp.float32, least / len(cuts), largest / len(cuts)))
        loudness = loudness * jnp.repeat(steps, shape[position] // parts).reshape([-1 if axis == position else 1 for axis in range(len(shape))])
    return loudness


def gaussian(rng, dims, spread, reach, split=(), held_as=jnp.bfloat16):
    array = jax.random.normal(rng, dims, jnp.float32) * spread
    if len(split) > 0:
        array = block_scale(rng, dims, split, -0.22, 0.18) * array
    return jnp.clip(array, min=-reach, max=reach).astype(held_as)


def setup_inputs(seed: int = 0) -> dict:
    keys = jax.random.split(jax.random.key(seed), 4)
    return {
        "weights": gaussian(keys[0], (NL, C, 9 * C), (9 * C) ** -0.5, 0.375, ((0, 8),)),
        "image": gaussian(keys[1], (B, C, IMG_ROWS, IMG_W), 1.0, 6.0, ((2, 4),), jnp.float32),
        "guess": gaussian(keys[2], (K, B, C, IMG_ROWS, IMG_W), 1.0, 6.0, ((0, 8), (3, 4)), jnp.float32),
    }


step_size = 0.125


def conv_layer(current, matrix):
    channels = current.shape[1]
    kernel = matrix.reshape(channels, 3, 3, channels).transpose(0, 3, 1, 2)
    return lax.conv_general_dilated(current.astype(jnp.bfloat16), kernel, (1, 1), ((1, 1), (1, 1)), dimension_numbers=("NCHW", "OIHW", "NCHW"), preferred_element_type=jnp.float32)


def reference(weights, image, guess):
    layers_all = L_DEV * N_LAYER
    points = layers_all // M
    stride = step_size
    grouped = weights.reshape(points, M, C, 9 * C)
    anchors = jnp.concatenate([image[None], guess[:-1]], axis=0)

    def interval(inputs):
        anchor, layer_w = inputs
        opening = conv_layer(anchor, layer_w[0])
        current = anchor + stride * jnp.tanh(opening)
        for j in range(1, M):
            current = current + stride * jnp.tanh(conv_layer(current, layer_w[j]))
        return current - (anchor + (M * stride) * jnp.tanh(opening))

    defects = lax.map(interval, (anchors, grouped))

    def advance(current, inputs):
        layer_w, defect = inputs
        updated = current + (M * stride) * jnp.tanh(conv_layer(current, layer_w)) + defect
        return updated, updated

    _, corrected = lax.scan(advance, image, (grouped[:, 0], defects))
    return corrected
```

```python
import functools

import jax
import jax.numpy as jnp
from jax import lax
from jax.experimental import pallas as pl
from jax.experimental.pallas import tpu as pltpu
from jax.sharding import PartitionSpec as P

M = 4
LEVELS = 2
STEP = 0.125
GROUP = 6
MESH = pl.DeviceIdType.MESH
F32 = jnp.float32
BF16 = jnp.bfloat16


def groups(low, high):
    found = []
    start = low
    while start < high:
        first = min(start, high - GROUP)
        found.append((first, start - first))
        start += GROUP
    return found


def chunks(low, high):
    return [(start, min(start + GROUP, high)) for start in range(low, high, GROUP)]


def put(patches, start, value):
    count, channels, breadth = value.shape
    flat = value.reshape(count * channels, breadth)
    column = lax.broadcasted_iota(jnp.int32, flat.shape, 1)
    left = jnp.where(column == 0, 0.0, pltpu.roll(flat, 1, 1))
    right = jnp.where(column == breadth - 1, 0.0, pltpu.roll(flat, breadth - 1, 1))
    rows = pl.ds(start, count)
    for place, part in enumerate((left, flat, right)):
        patches[rows, place * channels : (place + 1) * channels, :] = part.reshape(value.shape).astype(BF16)


def conv(matrix_ref, layer, patches, start, skip):
    window = patches[start - 1 : start + GROUP + 1]
    channels = window.shape[1] // 3
    flat = window.reshape(window.shape[0] * window.shape[1], window.shape[2])
    product = jnp.dot(matrix_ref[layer, skip * channels :, :], flat, preferred_element_type=F32)
    return product.reshape(GROUP - skip, channels, window.shape[2])


def masked(value, low, first, last, above, below):
    high = low + value.shape[0]
    parts = []
    if low < first:
        parts.append(value[: min(first, high) - low] * above)
    if max(low, first) < min(high, last):
        parts.append(value[max(low, first) - low : min(high, last) - low])
    if high > last:
        parts.append(value[max(low, last) - low :] * below)
    return parts[0] if len(parts) == 1 else jnp.concatenate(parts, axis=0)


def cycle_kernel(
    sections, bands, matrix, guess, image, out,
    wide0, wide1, entry, leave, state0, state1, patch0, patch1, defect0, defect1,
    start_send, start_recv, chain_send, chain_recv,
):
    batch, height = image.shape[0], image.shape[1]
    s = lax.axis_index("layer")
    r = lax.axis_index("rows")
    above = jnp.where(r > 0, 1.0, 0.0).astype(F32)
    below = jnp.where(r < bands - 1, 1.0, 0.0).astype(F32)
    deep0, deep1, near = M + 1, M, LEVELS

    has = {
        (i, j): functools.reduce(
            jnp.logical_and,
            [c for c in (
                s > 0 if i < 0 else (s < sections - 1 if i > 0 else None),
                r > 0 if j < 0 else (r < bands - 1 if j > 0 else None),
            ) if c is not None],
        )
        for i in (-1, 0, 1) for j in (-1, 0, 1) if (i, j) != (0, 0)
    }

    barrier = pltpu.get_barrier_semaphore()
    total = 0
    for (i, j), there in has.items():
        @pl.when(there)
        def _(i=i, j=j):
            pl.semaphore_signal(barrier, inc=1, device_id=(s + i, r + j), device_id_type=MESH)
        total = total + there.astype(jnp.int32)
    pl.semaphore_wait(barrier, total)

    def start_copy(source, target, slot, img, i, j):
        return pltpu.make_async_remote_copy(
            src_ref=source, dst_ref=target,
            send_sem=start_send.at[slot, img], recv_sem=start_recv.at[slot, img],
            device_id=(s + i, r + j), device_id_type=MESH,
        )

    def band0(img):
        return start_copy(guess.at[1, img], wide0.at[img, pl.ds(deep0, height)], 0, img, 1, 0)

    def down0(img, own):
        source = image.at[img] if own else guess.at[1, img]
        return start_copy(
            source.at[pl.ds(height - deep0, deep0)], wide0.at[img, pl.ds(0, deep0)],
            5 if own else 1, img, 0 if own else 1, 1)

    def up0(img, own):
        source = image.at[img] if own else guess.at[1, img]
        return start_copy(
            source.at[pl.ds(0, deep0)], wide0.at[img, pl.ds(deep0 + height, deep0)],
            6 if own else 2, img, 0 if own else 1, -1)

    def down1(img):
        return start_copy(
            guess.at[0, img, pl.ds(height - deep1, deep1)], wide1.at[img, pl.ds(0, deep1)], 3, img, 0, 1)

    def up1(img):
        return start_copy(
            guess.at[0, img, pl.ds(0, deep1)], wide1.at[img, pl.ds(deep1 + height, deep1)], 4, img, 0, -1)

    first = s == 0
    plan = [
        (band0, s < sections - 1, s > 0),
        (functools.partial(down0, own=True), first & (r < bands - 1), first & (r > 0)),
        (functools.partial(up0, own=True), first & (r > 0), first & (r < bands - 1)),
        (functools.partial(down0, own=False), has[1, 1], has[-1, -1]),
        (functools.partial(up0, own=False), has[1, -1], has[-1, 1]),
        (down1, r < bands - 1, r > 0),
        (up1, r > 0, r < bands - 1),
    ]
    for img in range(batch):
        for copy, sends, _ in plan:
            @pl.when(sends)
            def _(img=img, copy=copy):
                copy(img).start()

    @pl.when(r == 0)
    def _():
        for img in range(batch):
            wide0[img, :deep0] = jnp.zeros((deep0,) + wide0.shape[2:], BF16)
            wide1[img, :deep1] = jnp.zeros((deep1,) + wide1.shape[2:], BF16)
            entry[img, :near] = jnp.zeros((near,) + entry.shape[2:], BF16)

    @pl.when(r == bands - 1)
    def _():
        for img in range(batch):
            wide0[img, deep0 + height :] = jnp.zeros((deep0,) + wide0.shape[2:], BF16)
            wide1[img, deep1 + height :] = jnp.zeros((deep1,) + wide1.shape[2:], BF16)
            entry[img, near + height :] = jnp.zeros((near,) + entry.shape[2:], BF16)

    for img in range(batch):
        wide1[img, deep1 : deep1 + height] = guess[0, img]

    @pl.when(first)
    def _():
        for img in range(batch):
            wide0[img, deep0 : deep0 + height] = image[img]

    def relax(img):
        for copy, _, receives in plan:
            @pl.when(receives)
            def _(copy=copy):
                copy(img).wait_recv()
        anchors = (
            (1, wide1, deep1, state1, patch1, defect1, 0),
            (0, wide0, deep0, state0, patch0, defect0, 1),
        )
        for _, wide, deep, state, patch, _, _ in anchors:
            for low, high in chunks(0, height + 2 * deep):
                value = wide[img, low:high].astype(F32)
                state[low:high] = value
                put(patch.at[0], low, value)
        for j in range(M):
            for point, _, deep, state, patch, defect, extra in anchors:
                end = deep + height
                for start, skip in groups(j + 1, end + deep - j - 1):
                    low, high = start + skip, start + GROUP
                    change = STEP * jnp.tanh(conv(matrix, point * M + j, patch.at[j % 2], start, skip))
                    old = state[low:high]
                    new = old + change
                    a, b = max(low, deep - extra), min(high, end + extra)
                    if a < b:
                        rows = pl.ds(a - deep + extra, b - a)
                        part = slice(a - low, b - low)
                        if j == 0:
                            defect[img, rows] = -(old + M * change)[part]
                        if j == M - 1:
                            defect[img, rows] = defect[img, rows] + new[part]
                    if j < M - 1:
                        new = masked(new, low, deep, end, above, below)
                        state[low:high] = new
                        put(patch.at[(j + 1) % 2], low, new)

    def chain_copy(source, target, slot, img, j):
        return pltpu.make_async_remote_copy(
            src_ref=leave.at[img, source], dst_ref=entry.at[img, target],
            send_sem=chain_send.at[slot, img], recv_sem=chain_recv.at[slot, img],
            device_id=(s + 1, r + j), device_id_type=MESH,
        )

    def hand_on(img):
        return (
            (chain_copy(pl.ds(height - near, near), pl.ds(0, near), 0, img, 1), has[1, 1], has[-1, -1]),
            (chain_copy(pl.ds(0, near), pl.ds(near + height, near), 1, img, -1), has[1, -1], has[-1, 1]),
            (chain_copy(pl.ds(0, height), pl.ds(near, height), 2, img, 0), has[1, 0], has[-1, 0]),
        )

    def coarse(img):
        for copy, _, receives in hand_on(img):
            @pl.when(receives)
            def _(copy=copy):
                copy.wait_recv()

        @pl.when(first)
        def _():
            entry[img] = wide0[img, deep0 - near : deep0 + height + near]

        end = near + height
        for low, high in chunks(0, end + near):
            value = entry[img, low:high].astype(F32)
            state0[low:high] = value
            put(patch0.at[0], low, value)
        for start, skip in groups(1, end + 1):
            low, high = start + skip, start + GROUP
            change = (M * STEP) * jnp.tanh(conv(matrix, 0, patch0.at[0], start, skip))
            new = (state0[low:high] + change) + defect0[img, low - 1 : high - 1]
            new = masked(new, low, near, end, above, below)
            state0[low:high] = new
            put(patch0.at[1], low, new)
            a, b = max(low, near), min(high, end)
            out[0, img, a - near : b - near] = new[a - low : b - low]
        for start, skip in groups(near, end):
            low, high = start + skip, start + GROUP
            change = (M * STEP) * jnp.tanh(conv(matrix, M, patch0.at[1], start, skip))
            rows = slice(low - near, high - near)
            new = (state0[low:high] + change) + defect1[img, rows]
            out[1, img, rows] = new
            leave[img, rows] = new.astype(BF16)
        for copy, sends, _ in hand_on(img):
            @pl.when(sends)
            def _(copy=copy):
                copy.start()

    def tick(t, carry):
        relaxes = jnp.where(first, t % 2 == 0, t < batch)
        img = jnp.where(first, t // 2, t % batch)

        @pl.when(relaxes)
        def _():
            relax(img)

        @pl.when(jnp.logical_not(relaxes))
        def _():
            coarse(img)

        return carry

    lax.fori_loop(0, 2 * batch, tick, 0)

    for img in range(batch):
        for copy, sends, _ in plan:
            @pl.when(sends)
            def _(img=img, copy=copy):
                copy(img).wait_send()
        for copy, sends, _ in hand_on(img):
            @pl.when(sends)
            def _(copy=copy):
                copy.wait_send()


def toeplitz(weights):
    tap = weights.shape[2] // 3
    return jnp.concatenate(
        [
            jnp.pad(weights, ((0, 0), (0, 0), (row * tap, (GROUP - 1 - row) * tap)))
            for row in range(GROUP)
        ],
        axis=1,
    )


def per_device(sections, bands, weights, image, guess):
    levels, batch, channels, height, breadth = guess.shape
    matrix = toeplitz(weights)
    moved = jnp.transpose(guess, (0, 1, 3, 2, 4)).astype(BF16)
    picture = jnp.transpose(image, (0, 2, 1, 3)).astype(BF16)
    rows0, rows1 = height + 2 * (M + 1), height + 2 * M
    plane = (channels, breadth)
    wide_plane = (3 * channels, breadth)
    result = pl.pallas_call(
        functools.partial(cycle_kernel, sections, bands),
        out_shape=jax.ShapeDtypeStruct((levels, batch, height) + plane, F32),
        in_specs=[pl.BlockSpec(memory_space=pltpu.VMEM)] * 3,
        out_specs=pl.BlockSpec(memory_space=pltpu.VMEM),
        scratch_shapes=[
            pltpu.VMEM((batch, rows0) + plane, BF16),
            pltpu.VMEM((batch, rows1) + plane, BF16),
            pltpu.VMEM((batch, height + 2 * LEVELS) + plane, BF16),
            pltpu.VMEM((batch, height) + plane, BF16),
            pltpu.VMEM((rows0,) + plane, F32),
            pltpu.VMEM((rows1,) + plane, F32),
            pltpu.VMEM((2, rows0) + wide_plane, BF16),
            pltpu.VMEM((2, rows1) + wide_plane, BF16),
            pltpu.VMEM((batch, height + 2) + plane, F32),
            pltpu.VMEM((batch, height) + plane, F32),
            pltpu.SemaphoreType.DMA((7, batch)),
            pltpu.SemaphoreType.DMA((7, batch)),
            pltpu.SemaphoreType.DMA((3, batch)),
            pltpu.SemaphoreType.DMA((3, batch)),
        ],
        compiler_params=pltpu.CompilerParams(
            collective_id=0, has_side_effects=True, vmem_limit_bytes=40 * 1024 * 1024
        ),
        cost_estimate=pl.CostEstimate(
            flops=2_000_000_000, bytes_accessed=8_000_000, transcendentals=2_500_000
        ),
    )(matrix, moved, picture)
    return jnp.transpose(result, (0, 1, 3, 2, 4))


def solution(mesh):
    sizes = dict(mesh.shape)
    return jax.shard_map(
        functools.partial(per_device, sizes["layer"], sizes["rows"]),
        mesh=mesh,
        in_specs=(
            P("layer", None, None),
            P(None, None, "rows", None),
            P("layer", None, None, "rows", None),
        ),
        out_specs=P("layer", None, None, "rows", None),
        check_vma=False,
    )
```

```python
import functools

import jax
import jax.numpy as jnp
from jax import lax
from jax.experimental import pallas as pl
from jax.experimental.pallas import tpu as pltpu
from jax.sharding import PartitionSpec as P

M = 4
LEVELS = 2
STEP = 0.125
GROUP = 6
MESH = pl.DeviceIdType.MESH
F32 = jnp.float32
BF16 = jnp.bfloat16


def pairs(low, high):
    count = high - low
    upper = -(-count // 4)
    lower = count // 2 - upper
    middle = low + 2 * upper
    return [(low, upper, low - 1, 0), (middle, lower, middle - 1 - (GROUP - lower), GROUP - lower)]


def chunks(low, high):
    return [(start, min(start + GROUP, high)) for start in range(low, high, GROUP)]


def put(patches, start, value):
    count, channels, breadth = value.shape
    flat = value.reshape(count * channels, breadth)
    column = lax.broadcasted_iota(jnp.int32, flat.shape, 1)
    left = jnp.where(column == 0, 0.0, pltpu.roll(flat, 1, 1))
    right = jnp.where(column == breadth - 1, 0.0, pltpu.roll(flat, breadth - 1, 1))
    rows = pl.ds(start, count)
    for place, part in enumerate((left, flat, right)):
        patches[rows, place * channels : (place + 1) * channels, :] = part.reshape(value.shape).astype(BF16)


def conv(matrix_ref, layer, patches, size, window, skip):
    depth, width, breadth = patches.shape
    channels = width // 3
    parts = [
        patches[window + k * size : window + k * size + GROUP + 2].reshape((GROUP + 2) * width, breadth)
        for k in range(2)
    ]
    rows = matrix_ref[layer, skip * channels : (skip + size) * channels, :]
    product = jnp.dot(rows, jnp.concatenate(parts, axis=1), preferred_element_type=F32)
    return [
        product[:, k * breadth : (k + 1) * breadth].reshape(size, channels, breadth) for k in range(2)
    ]


def masked(value, low, first, last, above, below):
    high = low + value.shape[0]
    parts = []
    if low < first:
        parts.append(value[: min(first, high) - low] * above)
    if max(low, first) < min(high, last):
        parts.append(value[max(low, first) - low : min(high, last) - low])
    if high > last:
        parts.append(value[max(low, last) - low :] * below)
    return parts[0] if len(parts) == 1 else jnp.concatenate(parts, axis=0)


def cycle_kernel(
    sections, bands, narrow, guess, image, out,
    matrix, wide0, wide1, entry, leave, state0, state1, patch0, patch1, defect0, defect1,
    start_send, start_recv, chain_send, chain_recv,
):
    batch, height = image.shape[0], image.shape[1]
    s = lax.axis_index("layer")
    r = lax.axis_index("rows")
    above = jnp.where(r > 0, 1.0, 0.0).astype(F32)
    below = jnp.where(r < bands - 1, 1.0, 0.0).astype(F32)
    deep0, deep1, near = M + 1, M, LEVELS

    has = {
        (i, j): functools.reduce(
            jnp.logical_and,
            [c for c in (
                s > 0 if i < 0 else (s < sections - 1 if i > 0 else None),
                r > 0 if j < 0 else (r < bands - 1 if j > 0 else None),
            ) if c is not None],
        )
        for i in (-1, 0, 1) for j in (-1, 0, 1) if (i, j) != (0, 0)
    }

    barrier = pltpu.get_barrier_semaphore()
    total = 0
    for (i, j), there in has.items():
        @pl.when(there)
        def _(i=i, j=j):
            pl.semaphore_signal(barrier, inc=1, device_id=(s + i, r + j), device_id_type=MESH)
        total = total + there.astype(jnp.int32)
    pl.semaphore_wait(barrier, total)

    def start_copy(source, target, slot, img, i, j):
        return pltpu.make_async_remote_copy(
            src_ref=source, dst_ref=target,
            send_sem=start_send.at[slot, img], recv_sem=start_recv.at[slot, img],
            device_id=(s + i, r + j), device_id_type=MESH,
        )

    def band0(img):
        return start_copy(guess.at[1, img], wide0.at[img, pl.ds(deep0, height)], 0, img, 1, 0)

    def down0(img, own):
        source = image.at[img] if own else guess.at[1, img]
        return start_copy(
            source.at[pl.ds(height - deep0, deep0)], wide0.at[img, pl.ds(0, deep0)],
            5 if own else 1, img, 0 if own else 1, 1)

    def up0(img, own):
        source = image.at[img] if own else guess.at[1, img]
        return start_copy(
            source.at[pl.ds(0, deep0)], wide0.at[img, pl.ds(deep0 + height, deep0)],
            6 if own else 2, img, 0 if own else 1, -1)

    def down1(img):
        return start_copy(
            guess.at[0, img, pl.ds(height - deep1, deep1)], wide1.at[img, pl.ds(0, deep1)], 3, img, 0, 1)

    def up1(img):
        return start_copy(
            guess.at[0, img, pl.ds(0, deep1)], wide1.at[img, pl.ds(deep1 + height, deep1)], 4, img, 0, -1)

    first = s == 0
    plan = [
        (band0, s < sections - 1, s > 0),
        (functools.partial(down0, own=True), first & (r < bands - 1), first & (r > 0)),
        (functools.partial(up0, own=True), first & (r > 0), first & (r < bands - 1)),
        (functools.partial(down0, own=False), has[1, 1], has[-1, -1]),
        (functools.partial(up0, own=False), has[1, -1], has[-1, 1]),
        (down1, r < bands - 1, r > 0),
        (up1, r > 0, r < bands - 1),
    ]
    for img in range(batch):
        for copy, sends, _ in plan:
            @pl.when(sends)
            def _(img=img, copy=copy):
                copy(img).start()

    @pl.when(r == 0)
    def _():
        for img in range(batch):
            wide0[img, :deep0] = jnp.zeros((deep0,) + wide0.shape[2:], BF16)
            wide1[img, :deep1] = jnp.zeros((deep1,) + wide1.shape[2:], BF16)
            entry[img, :near] = jnp.zeros((near,) + entry.shape[2:], BF16)

    @pl.when(r == bands - 1)
    def _():
        for img in range(batch):
            wide0[img, deep0 + height :] = jnp.zeros((deep0,) + wide0.shape[2:], BF16)
            wide1[img, deep1 + height :] = jnp.zeros((deep1,) + wide1.shape[2:], BF16)
            entry[img, near + height :] = jnp.zeros((near,) + entry.shape[2:], BF16)

    for img in range(batch):
        wide1[img, deep1 : deep1 + height] = guess[0, img]

    @pl.when(first)
    def _():
        for img in range(batch):
            wide0[img, deep0 : deep0 + height] = image[img]

    channels = narrow.shape[1]
    for layer in range(narrow.shape[0]):
        taps = narrow[layer].astype(F32)
        for k in range(GROUP):
            moved = taps if k == 0 else pltpu.roll(taps, k * 3 * channels, 1)
            matrix[layer, k * channels : (k + 1) * channels, :] = moved.astype(BF16)

    def convolved(layer, patches, low, high):
        for first_row, size, window, skip in pairs(low, high):
            for k, product in enumerate(conv(matrix, layer, patches, size, window, skip)):
                yield first_row + k * size, first_row + (k + 1) * size, product

    def relax(img):
        for copy, _, receives in plan:
            @pl.when(receives)
            def _(copy=copy):
                copy(img).wait_recv()
        anchors = (
            (1, wide1, deep1, state1, patch1, defect1, 0),
            (0, wide0, deep0, state0, patch0, defect0, 1),
        )
        for _, wide, deep, state, patch, _, _ in anchors:
            for low, high in chunks(0, height + 2 * deep):
                value = wide[img, low:high].astype(F32)
                state[low:high] = value
                put(patch.at[0], low, value)
        for j in range(M):
            for point, _, deep, state, patch, defect, extra in anchors:
                end = deep + height
                for low, high, product in convolved(point * M + j, patch.at[j % 2], j + 1, end + deep - j - 1):
                    change = STEP * jnp.tanh(product)
                    old = state[low:high]
                    new = old + change
                    a, b = max(low, deep - extra), min(high, end + extra)
                    if a < b:
                        rows = pl.ds(a - deep + extra, b - a)
                        part = slice(a - low, b - low)
                        if j == 0:
                            defect[img, rows] = -(old + M * change)[part]
                        if j == M - 1:
                            defect[img, rows] = defect[img, rows] + new[part]
                    if j < M - 1:
                        new = masked(new, low, deep, end, above, below)
                        state[low:high] = new
                        put(patch.at[(j + 1) % 2], low, new)

    def chain_copy(source, target, slot, img, j):
        return pltpu.make_async_remote_copy(
            src_ref=leave.at[img, source], dst_ref=entry.at[img, target],
            send_sem=chain_send.at[slot, img], recv_sem=chain_recv.at[slot, img],
            device_id=(s + 1, r + j), device_id_type=MESH,
        )

    def hand_on(img):
        half = height // 2
        return (
            (chain_copy(pl.ds(0, near), pl.ds(near + height, near), 0, img, -1), has[1, -1], has[-1, 1], near),
            (chain_copy(pl.ds(0, half), pl.ds(near, half), 1, img, 0), has[1, 0], has[-1, 0], half),
            (chain_copy(pl.ds(height - near, near), pl.ds(0, near), 2, img, 1), has[1, 1], has[-1, -1], height),
            (chain_copy(pl.ds(half, height - half), pl.ds(near + half, height - half), 3, img, 0),
             has[1, 0], has[-1, 0], height),
        )

    def coarse(img):
        for copy, _, receives, _ in hand_on(img):
            @pl.when(receives)
            def _(copy=copy):
                copy.wait_recv()

        @pl.when(first)
        def _():
            entry[img] = wide0[img, deep0 - near : deep0 + height + near]

        end = near + height
        for low, high in chunks(0, end + near):
            value = entry[img, low:high].astype(F32)
            state0[low:high] = value
            put(patch0.at[0], low, value)
        for low, high, product in convolved(0, patch0.at[0], 1, end + 1):
            change = (M * STEP) * jnp.tanh(product)
            new = (state0[low:high] + change) + defect0[img, low - 1 : high - 1]
            new = masked(new, low, near, end, above, below)
            state0[low:high] = new
            put(patch0.at[1], low, new)
            a, b = max(low, near), min(high, end)
            out[0, img, a - near : b - near] = new[a - low : b - low]
        ready = list(hand_on(img))
        for low, high, product in convolved(M, patch0.at[1], near, end):
            change = (M * STEP) * jnp.tanh(product)
            rows = slice(low - near, high - near)
            new = (state0[low:high] + change) + defect1[img, rows]
            out[1, img, rows] = new
            leave[img, rows] = new.astype(BF16)
            while ready and ready[0][3] <= high - near:
                copy, sends, _, _ = ready.pop(0)

                @pl.when(sends)
                def _(copy=copy):
                    copy.start()

    def tick(t, carry):
        relaxes = jnp.where(first, t % 2 == 0, t < batch)
        img = jnp.where(first, t // 2, t % batch)

        @pl.when(relaxes)
        def _():
            relax(img)

        @pl.when(jnp.logical_not(relaxes))
        def _():
            coarse(img)

        return carry

    lax.fori_loop(0, 2 * batch, tick, 0)

    for img in range(batch):
        for copy, sends, _ in plan:
            @pl.when(sends)
            def _(img=img, copy=copy):
                copy(img).wait_send()
        for copy, sends, _, _ in hand_on(img):
            @pl.when(sends)
            def _(copy=copy):
                copy.wait_send()


def per_device(sections, bands, weights, image, guess):
    levels, batch, channels, height, breadth = guess.shape
    window = (GROUP + 2) * 3 * channels
    narrow = jnp.pad(weights, ((0, 0), (0, 0), (0, window - weights.shape[2])))
    moved = jnp.transpose(guess, (0, 1, 3, 2, 4)).astype(BF16)
    picture = jnp.transpose(image, (0, 2, 1, 3)).astype(BF16)
    rows0, rows1 = height + 2 * (M + 1), height + 2 * M
    plane = (channels, breadth)
    wide_plane = (3 * channels, breadth)
    result = pl.pallas_call(
        functools.partial(cycle_kernel, sections, bands),
        out_shape=jax.ShapeDtypeStruct((levels, batch, height) + plane, F32),
        in_specs=[pl.BlockSpec(memory_space=pltpu.VMEM)] * 3,
        out_specs=pl.BlockSpec(memory_space=pltpu.VMEM),
        scratch_shapes=[
            pltpu.VMEM((weights.shape[0], GROUP * channels, window), BF16),
            pltpu.VMEM((batch, rows0) + plane, BF16),
            pltpu.VMEM((batch, rows1) + plane, BF16),
            pltpu.VMEM((batch, height + 2 * LEVELS) + plane, BF16),
            pltpu.VMEM((batch, height) + plane, BF16),
            pltpu.VMEM((rows0,) + plane, F32),
            pltpu.VMEM((rows1,) + plane, F32),
            pltpu.VMEM((2, rows0) + wide_plane, BF16),
            pltpu.VMEM((2, rows1) + wide_plane, BF16),
            pltpu.VMEM((batch, height + 2) + plane, F32),
            pltpu.VMEM((batch, height) + plane, F32),
            pltpu.SemaphoreType.DMA((7, batch)),
            pltpu.SemaphoreType.DMA((7, batch)),
            pltpu.SemaphoreType.DMA((4, batch)),
            pltpu.SemaphoreType.DMA((4, batch)),
        ],
        compiler_params=pltpu.CompilerParams(
            collective_id=0, has_side_effects=True, vmem_limit_bytes=40 * 1024 * 1024
        ),
        cost_estimate=pl.CostEstimate(
            flops=2_000_000_000, bytes_accessed=8_000_000, transcendentals=2_500_000
        ),
    )(narrow, moved, picture)
    return jnp.transpose(result, (0, 1, 3, 2, 4))


def solution(mesh):
    sizes = dict(mesh.shape)
    return jax.shard_map(
        functools.partial(per_device, sizes["layer"], sizes["rows"]),
        mesh=mesh,
        in_specs=(
            P("layer", None, None),
            P(None, None, "rows", None),
            P("layer", None, None, "rows", None),
        ),
        out_specs=P("layer", None, None, "rows", None),
        check_vma=False,
    )
```

```python
import functools

import jax
import jax.numpy as jnp
from jax import lax
from jax.experimental import pallas as pl
from jax.experimental.pallas import tpu as pltpu
from jax.sharding import PartitionSpec as P

M = 4
LEVELS = 2
STEP = 0.125
GROUP = 6
MESH = pl.DeviceIdType.MESH
F32 = jnp.float32
BF16 = jnp.bfloat16


def pairs(low, high):
    count = high - low
    upper = -(-count // 4)
    lower = count // 2 - upper
    middle = low + 2 * upper
    return [(low, upper, low - 1, 0), (middle, lower, middle - 1 - (GROUP - lower), GROUP - lower)]


def chunks(low, high):
    return [(start, min(start + GROUP, high)) for start in range(low, high, GROUP)]


def put(patches, start, value):
    count, channels, breadth = value.shape
    flat = value.reshape(count * channels, breadth)
    column = lax.broadcasted_iota(jnp.int32, flat.shape, 1)
    left = jnp.where(column == 0, 0.0, pltpu.roll(flat, 1, 1))
    right = jnp.where(column == breadth - 1, 0.0, pltpu.roll(flat, breadth - 1, 1))
    rows = pl.ds(start, count)
    for place, part in enumerate((left, flat, right)):
        patches[rows, place * channels : (place + 1) * channels, :] = part.reshape(value.shape).astype(BF16)


def conv(matrix_ref, layer, patches, size, window, skip):
    depth, width, breadth = patches.shape
    channels = width // 3
    parts = [
        patches[window + k * size : window + k * size + GROUP + 2].reshape((GROUP + 2) * width, breadth)
        for k in range(2)
    ]
    rows = matrix_ref[layer, skip * channels : (skip + size) * channels, :]
    product = jnp.dot(rows, jnp.concatenate(parts, axis=1), preferred_element_type=F32)
    return [
        product[:, k * breadth : (k + 1) * breadth].reshape(size, channels, breadth) for k in range(2)
    ]


def masked(value, low, first, last, above, below):
    high = low + value.shape[0]
    parts = []
    if low < first:
        parts.append(value[: min(first, high) - low] * above)
    if max(low, first) < min(high, last):
        parts.append(value[max(low, first) - low : min(high, last) - low])
    if high > last:
        parts.append(value[max(low, last) - low :] * below)
    return parts[0] if len(parts) == 1 else jnp.concatenate(parts, axis=0)


def cycle_kernel(
    sections, bands, narrow, guess, image, out,
    matrix, padded, wide0, wide1, entry, leave, state, patch, state0, patch0, defect0, defect1,
    start_send, start_recv, chain_send, chain_recv,
):
    batch, height = image.shape[0], image.shape[1]
    s = lax.axis_index("layer")
    r = lax.axis_index("rows")
    above = jnp.where(r > 0, 1.0, 0.0).astype(F32)
    below = jnp.where(r < bands - 1, 1.0, 0.0).astype(F32)
    deep0, deep1, near = M + 1, M, LEVELS

    has = {
        (i, j): functools.reduce(
            jnp.logical_and,
            [c for c in (
                s > 0 if i < 0 else (s < sections - 1 if i > 0 else None),
                r > 0 if j < 0 else (r < bands - 1 if j > 0 else None),
            ) if c is not None],
        )
        for i in (-1, 0, 1) for j in (-1, 0, 1) if (i, j) != (0, 0)
    }

    barrier = pltpu.get_barrier_semaphore()
    total = 0
    for (i, j), there in has.items():
        @pl.when(there)
        def _(i=i, j=j):
            pl.semaphore_signal(barrier, inc=1, device_id=(s + i, r + j), device_id_type=MESH)
        total = total + there.astype(jnp.int32)
    pl.semaphore_wait(barrier, total)

    def start_copy(source, target, slot, i, j):
        return pltpu.make_async_remote_copy(
            src_ref=source, dst_ref=target,
            send_sem=start_send.at[slot], recv_sem=start_recv.at[slot],
            device_id=(s + i, r + j), device_id_type=MESH,
        )

    def edge(source, wide, depth, slot, i, j):
        origin, target = (height - depth, 0) if j > 0 else (0, depth + height)
        return start_copy(
            source.at[:, pl.ds(origin, depth)], wide.at[:, pl.ds(target, depth)], slot, i, j)

    first = s == 0
    plan = [
        (edge(guess.at[0], wide1, deep1, 0, 0, 1), r < bands - 1, r > 0, 1),
        (edge(guess.at[0], wide1, deep1, 1, 0, -1), r > 0, r < bands - 1, 1),
        (start_copy(guess.at[1], wide0.at[:, pl.ds(deep0, height)], 2, 1, 0), s < sections - 1, s > 0, 0),
        (edge(guess.at[1], wide0, deep0, 3, 1, 1), has[1, 1], has[-1, -1], 0),
        (edge(guess.at[1], wide0, deep0, 4, 1, -1), has[1, -1], has[-1, 1], 0),
        (edge(image, wide0, deep0, 5, 0, 1), first & (r < bands - 1), first & (r > 0), 0),
        (edge(image, wide0, deep0, 6, 0, -1), first & (r > 0), first & (r < bands - 1), 0),
    ]
    for copy, sends, _, _ in plan:
        @pl.when(sends)
        def _(copy=copy):
            copy.start()

    @pl.when(r == 0)
    def _():
        for img in range(batch):
            wide0[img, :deep0] = jnp.zeros((deep0,) + wide0.shape[2:], BF16)
            wide1[img, :deep1] = jnp.zeros((deep1,) + wide1.shape[2:], BF16)
            entry[img, :near] = jnp.zeros((near,) + entry.shape[2:], BF16)

    @pl.when(r == bands - 1)
    def _():
        for img in range(batch):
            wide0[img, deep0 + height :] = jnp.zeros((deep0,) + wide0.shape[2:], BF16)
            wide1[img, deep1 + height :] = jnp.zeros((deep1,) + wide1.shape[2:], BF16)
            entry[img, near + height :] = jnp.zeros((near,) + entry.shape[2:], BF16)

    for img in range(batch):
        wide1[img, deep1 : deep1 + height] = guess[0, img]

    @pl.when(first)
    def _():
        for img in range(batch):
            wide0[img, deep0 : deep0 + height] = image[img]

    channels = narrow.shape[1]
    padded[...] = jnp.zeros(padded.shape, F32)
    for layer in range(narrow.shape[0]):
        padded[layer, :, : narrow.shape[2]] = narrow[layer].astype(F32)
        taps = padded[layer]
        for k in range(GROUP):
            moved = taps if k == 0 else pltpu.roll(taps, k * 3 * channels, 1)
            matrix[layer, k * channels : (k + 1) * channels, :] = moved.astype(BF16)

    def convolved(layer, patches, low, high):
        for first_row, size, window, skip in pairs(low, high):
            for k, product in enumerate(conv(matrix, layer, patches, size, window, skip)):
                yield first_row + k * size, first_row + (k + 1) * size, product

    breadth = image.shape[3]

    def lanes(img):
        return pl.ds(img * breadth, breadth)

    def relax(point):
        wide, deep, defect, extra = ((wide0, deep0, defect0, 1), (wide1, deep1, defect1, 0))[point]
        for copy, _, receives, needed in plan:
            if needed == point:
                @pl.when(receives)
                def _(copy=copy):
                    copy.wait_recv()
        end = deep + height
        for img in range(batch):
            for low, high in chunks(0, end + deep):
                value = wide[img, low:high].astype(F32)
                state[low:high, :, lanes(img)] = value
                put(patch.at[0, :, :, lanes(img)], low, value)
        for j in range(M):
            for low, high, product in convolved(point * M + j, patch.at[j % 2], j + 1, end + deep - j - 1):
                change = STEP * jnp.tanh(product)
                old = state[low:high]
                new = old + change
                a, b = max(low, deep - extra), min(high, end + extra)
                if a < b:
                    rows = pl.ds(a - deep + extra, b - a)
                    part = slice(a - low, b - low)
                    if j == 0:
                        defect[rows] = -(old + M * change)[part]
                    if j == M - 1:
                        defect[rows] = defect[rows] + new[part]
                if j < M - 1:
                    new = masked(new, low, deep, end, above, below)
                    state[low:high] = new
                    for img in range(batch):
                        own = new[:, :, img * breadth : (img + 1) * breadth]
                        put(patch.at[(j + 1) % 2, :, :, lanes(img)], low, own)

    def chain_copy(source, target, slot, img, j):
        return pltpu.make_async_remote_copy(
            src_ref=leave.at[img, source], dst_ref=entry.at[img, target],
            send_sem=chain_send.at[slot, img], recv_sem=chain_recv.at[slot, img],
            device_id=(s + 1, r + j), device_id_type=MESH,
        )

    def hand_on(img):
        return (
            (chain_copy(pl.ds(height - near, near), pl.ds(0, near), 0, img, 1), has[1, 1], has[-1, -1]),
            (chain_copy(pl.ds(0, near), pl.ds(near + height, near), 1, img, -1), has[1, -1], has[-1, 1]),
            (chain_copy(pl.ds(0, height), pl.ds(near, height), 2, img, 0), has[1, 0], has[-1, 0]),
        )

    def coarse(img):
        column = pl.ds(pl.multiple_of(img * breadth, breadth), breadth)
        for copy, _, receives in hand_on(img):
            @pl.when(receives)
            def _(copy=copy):
                copy.wait_recv()

        @pl.when(first)
        def _():
            entry[img] = wide0[img, deep0 - near : deep0 + height + near]

        end = near + height
        for low, high in chunks(0, end + near):
            value = entry[img, low:high].astype(F32)
            state0[low:high] = value
            put(patch0.at[0], low, value)
        for low, high, product in convolved(0, patch0.at[0], 1, end + 1):
            change = (M * STEP) * jnp.tanh(product)
            new = (state0[low:high] + change) + defect0[low - 1 : high - 1, :, column]
            new = masked(new, low, near, end, above, below)
            state0[low:high] = new
            put(patch0.at[1], low, new)
            a, b = max(low, near), min(high, end)
            out[0, img, a - near : b - near] = new[a - low : b - low]
        for low, high, product in convolved(M, patch0.at[1], near, end):
            change = (M * STEP) * jnp.tanh(product)
            rows = slice(low - near, high - near)
            new = (state0[low:high] + change) + defect1[rows, :, column]
            out[1, img, rows] = new
            leave[img, rows] = new.astype(BF16)
        for copy, sends, _ in hand_on(img):
            @pl.when(sends)
            def _(copy=copy):
                copy.start()

    for point in range(LEVELS - 1, -1, -1):
        relax(point)

    def link(img, carry):
        coarse(img)
        return carry

    lax.fori_loop(0, batch, link, 0)

    for copy, sends, _, _ in plan:
        @pl.when(sends)
        def _(copy=copy):
            copy.wait_send()

    for img in range(batch):
        for copy, sends, _ in hand_on(img):
            @pl.when(sends)
            def _(copy=copy):
                copy.wait_send()


def per_device(sections, bands, weights, image, guess):
    levels, batch, channels, height, breadth = guess.shape
    window = (GROUP + 2) * 3 * channels
    moved = jnp.transpose(guess, (0, 1, 3, 2, 4)).astype(BF16)
    picture = jnp.transpose(image, (0, 2, 1, 3)).astype(BF16)
    rows0, rows1 = height + 2 * (M + 1), height + 2 * M
    plane = (channels, breadth)
    wide_plane = (3 * channels, breadth)
    result = pl.pallas_call(
        functools.partial(cycle_kernel, sections, bands),
        out_shape=jax.ShapeDtypeStruct((levels, batch, height) + plane, F32),
        in_specs=[pl.BlockSpec(memory_space=pltpu.VMEM)] * 3,
        out_specs=pl.BlockSpec(memory_space=pltpu.VMEM),
        scratch_shapes=[
            pltpu.VMEM((weights.shape[0], GROUP * channels, window), BF16),
            pltpu.VMEM((weights.shape[0], channels, window), F32),
            pltpu.VMEM((batch, rows0) + plane, BF16),
            pltpu.VMEM((batch, rows1) + plane, BF16),
            pltpu.VMEM((batch, height + 2 * LEVELS) + plane, BF16),
            pltpu.VMEM((batch, height) + plane, BF16),
            pltpu.VMEM((rows0, channels, batch * breadth), F32),
            pltpu.VMEM((2, rows0, 3 * channels, batch * breadth), BF16),
            pltpu.VMEM((height + 2 * LEVELS,) + plane, F32),
            pltpu.VMEM((2, height + 2 * LEVELS) + wide_plane, BF16),
            pltpu.VMEM((height + 2, channels, batch * breadth), F32),
            pltpu.VMEM((height, channels, batch * breadth), F32),
            pltpu.SemaphoreType.DMA((7,)),
            pltpu.SemaphoreType.DMA((7,)),
            pltpu.SemaphoreType.DMA((3, batch)),
            pltpu.SemaphoreType.DMA((3, batch)),
        ],
        compiler_params=pltpu.CompilerParams(
            collective_id=0, has_side_effects=True, vmem_limit_bytes=40 * 1024 * 1024
        ),
        cost_estimate=pl.CostEstimate(
            flops=2_000_000_000, bytes_accessed=8_000_000, transcendentals=2_500_000
        ),
    )(weights, moved, picture)
    return jnp.transpose(result, (0, 1, 3, 2, 4))


def solution(mesh):
    sizes = dict(mesh.shape)
    return jax.shard_map(
        functools.partial(per_device, sizes["layer"], sizes["rows"]),
        mesh=mesh,
        in_specs=(
            P("layer", None, None),
            P(None, None, "rows", None),
            P("layer", None, None, "rows", None),
        ),
        out_specs=P("layer", None, None, "rows", None),
        check_vma=False,
    )
```

```python
import functools

import jax
import jax.numpy as jnp
from jax import lax
from jax.experimental import pallas as pl
from jax.experimental.pallas import tpu as pltpu
from jax.sharding import PartitionSpec as P

M = 4
LEVELS = 2
STEP = 0.125
GROUP = 6
MESH = pl.DeviceIdType.MESH
F32 = jnp.float32
BF16 = jnp.bfloat16


def pairs(low, high):
    count = high - low
    upper = -(-count // 4)
    lower = count // 2 - upper
    middle = low + 2 * upper
    return [(low, upper, low - 1, 0), (middle, lower, middle - 1 - (GROUP - lower), GROUP - lower)]


def chunks(low, high):
    return [(start, min(start + GROUP, high)) for start in range(low, high, GROUP)]


def conv(matrix_ref, layer, state, size, window, skip):
    channels, breadth = state.shape[1:]
    parts = [
        state[window + k * size : window + k * size + GROUP + 2].reshape((GROUP + 2) * channels, breadth)
        for k in range(2)
    ]
    count = size * channels
    rows = [matrix_ref[layer, tap, skip * channels : skip * channels + count, :] for tap in range(3)]
    product = jnp.dot(
        jnp.concatenate(rows, axis=0), jnp.concatenate(parts, axis=1), preferred_element_type=F32
    )
    column = lax.broadcasted_iota(jnp.int32, (count, breadth), 1)
    results = []
    for k in range(2):
        left, middle, right = (
            product[tap * count : (tap + 1) * count, k * breadth : (k + 1) * breadth] for tap in range(3)
        )
        left = jnp.where(column == 0, 0.0, pltpu.roll(left, 1, 1))
        right = jnp.where(column == breadth - 1, 0.0, pltpu.roll(right, breadth - 1, 1))
        results.append((left + middle + right).reshape(size, channels, breadth))
    return results


def masked(value, low, first, last, above, below):
    high = low + value.shape[0]
    parts = []
    if low < first:
        parts.append(value[: min(first, high) - low] * above)
    if max(low, first) < min(high, last):
        parts.append(value[max(low, first) - low : min(high, last) - low])
    if high > last:
        parts.append(value[max(low, last) - low :] * below)
    return parts[0] if len(parts) == 1 else jnp.concatenate(parts, axis=0)


def cycle_kernel(
    sections, bands, narrow, guess, image, out,
    matrix, wide0, wide1, entry, leave, state0, state1, patch0, patch1, defect0, defect1,
    start_send, start_recv, chain_send, chain_recv,
):
    batch, height = image.shape[0], image.shape[1]
    s = lax.axis_index("layer")
    r = lax.axis_index("rows")
    above = jnp.where(r > 0, 1.0, 0.0).astype(F32)
    below = jnp.where(r < bands - 1, 1.0, 0.0).astype(F32)
    deep0, deep1, near = M + 1, M, LEVELS

    has = {
        (i, j): functools.reduce(
            jnp.logical_and,
            [c for c in (
                s > 0 if i < 0 else (s < sections - 1 if i > 0 else None),
                r > 0 if j < 0 else (r < bands - 1 if j > 0 else None),
            ) if c is not None],
        )
        for i in (-1, 0, 1) for j in (-1, 0, 1) if (i, j) != (0, 0)
    }

    barrier = pltpu.get_barrier_semaphore()
    total = 0
    for (i, j), there in has.items():
        @pl.when(there)
        def _(i=i, j=j):
            pl.semaphore_signal(barrier, inc=1, device_id=(s + i, r + j), device_id_type=MESH)
        total = total + there.astype(jnp.int32)
    pl.semaphore_wait(barrier, total)

    def start_copy(source, target, slot, img, i, j):
        return pltpu.make_async_remote_copy(
            src_ref=source, dst_ref=target,
            send_sem=start_send.at[slot, img], recv_sem=start_recv.at[slot, img],
            device_id=(s + i, r + j), device_id_type=MESH,
        )

    def band0(img):
        return start_copy(guess.at[1, img], wide0.at[img, pl.ds(deep0, height)], 0, img, 1, 0)

    def down0(img, own):
        source = image.at[img] if own else guess.at[1, img]
        return start_copy(
            source.at[pl.ds(height - deep0, deep0)], wide0.at[img, pl.ds(0, deep0)],
            5 if own else 1, img, 0 if own else 1, 1)

    def up0(img, own):
        source = image.at[img] if own else guess.at[1, img]
        return start_copy(
            source.at[pl.ds(0, deep0)], wide0.at[img, pl.ds(deep0 + height, deep0)],
            6 if own else 2, img, 0 if own else 1, -1)

    def down1(img):
        return start_copy(
            guess.at[0, img, pl.ds(height - deep1, deep1)], wide1.at[img, pl.ds(0, deep1)], 3, img, 0, 1)

    def up1(img):
        return start_copy(
            guess.at[0, img, pl.ds(0, deep1)], wide1.at[img, pl.ds(deep1 + height, deep1)], 4, img, 0, -1)

    first = s == 0
    plan = [
        (band0, s < sections - 1, s > 0),
        (functools.partial(down0, own=True), first & (r < bands - 1), first & (r > 0)),
        (functools.partial(up0, own=True), first & (r > 0), first & (r < bands - 1)),
        (functools.partial(down0, own=False), has[1, 1], has[-1, -1]),
        (functools.partial(up0, own=False), has[1, -1], has[-1, 1]),
        (down1, r < bands - 1, r > 0),
        (up1, r > 0, r < bands - 1),
    ]
    for img in range(batch):
        for copy, sends, _ in plan:
            @pl.when(sends)
            def _(img=img, copy=copy):
                copy(img).start()

    @pl.when(r == 0)
    def _():
        for img in range(batch):
            wide0[img, :deep0] = jnp.zeros((deep0,) + wide0.shape[2:], BF16)
            wide1[img, :deep1] = jnp.zeros((deep1,) + wide1.shape[2:], BF16)
            entry[img, :near] = jnp.zeros((near,) + entry.shape[2:], BF16)

    @pl.when(r == bands - 1)
    def _():
        for img in range(batch):
            wide0[img, deep0 + height :] = jnp.zeros((deep0,) + wide0.shape[2:], BF16)
            wide1[img, deep1 + height :] = jnp.zeros((deep1,) + wide1.shape[2:], BF16)
            entry[img, near + height :] = jnp.zeros((near,) + entry.shape[2:], BF16)

    for img in range(batch):
        wide1[img, deep1 : deep1 + height] = guess[0, img]

    @pl.when(first)
    def _():
        for img in range(batch):
            wide0[img, deep0 : deep0 + height] = image[img]

    channels = narrow.shape[2]
    for layer in range(narrow.shape[0]):
        for tap in range(3):
            taps = narrow[layer, tap].astype(F32)
            for k in range(GROUP):
                moved = taps if k == 0 else pltpu.roll(taps, k * channels, 1)
                matrix[layer, tap, k * channels : (k + 1) * channels, :] = moved.astype(BF16)

    def convolved(layer, patches, low, high):
        for first_row, size, window, skip in pairs(low, high):
            for k, product in enumerate(conv(matrix, layer, patches, size, window, skip)):
                yield first_row + k * size, first_row + (k + 1) * size, product

    def relax(img):
        for copy, _, receives in plan:
            @pl.when(receives)
            def _(copy=copy):
                copy(img).wait_recv()
        anchors = (
            (1, wide1, deep1, state1, patch1, defect1, 0),
            (0, wide0, deep0, state0, patch0, defect0, 1),
        )
        for _, wide, deep, state, patch, _, _ in anchors:
            for low, high in chunks(0, height + 2 * deep):
                value = wide[img, low:high].astype(F32)
                state[low:high] = value
                patch[0, low:high] = value.astype(BF16)
        for j in range(M):
            for point, _, deep, state, patch, defect, extra in anchors:
                end = deep + height
                for low, high, product in convolved(point * M + j, patch.at[j % 2], j + 1, end + deep - j - 1):
                    change = STEP * jnp.tanh(product)
                    old = state[low:high]
                    new = old + change
                    a, b = max(low, deep - extra), min(high, end + extra)
                    if a < b:
                        rows = pl.ds(a - deep + extra, b - a)
                        part = slice(a - low, b - low)
                        if j == 0:
                            defect[img, rows] = -(old + M * change)[part]
                        if j == M - 1:
                            defect[img, rows] = defect[img, rows] + new[part]
                    if j < M - 1:
                        new = masked(new, low, deep, end, above, below)
                        state[low:high] = new
                        patch[(j + 1) % 2, low:high] = new.astype(BF16)

    def chain_copy(source, target, slot, img, j):
        return pltpu.make_async_remote_copy(
            src_ref=leave.at[img, source], dst_ref=entry.at[img, target],
            send_sem=chain_send.at[slot, img], recv_sem=chain_recv.at[slot, img],
            device_id=(s + 1, r + j), device_id_type=MESH,
        )

    def hand_on(img):
        half = height // 2
        return (
            (chain_copy(pl.ds(0, near), pl.ds(near + height, near), 0, img, -1), has[1, -1], has[-1, 1], near),
            (chain_copy(pl.ds(0, half), pl.ds(near, half), 1, img, 0), has[1, 0], has[-1, 0], half),
            (chain_copy(pl.ds(height - near, near), pl.ds(0, near), 2, img, 1), has[1, 1], has[-1, -1], height),
            (chain_copy(pl.ds(half, height - half), pl.ds(near + half, height - half), 3, img, 0),
             has[1, 0], has[-1, 0], height),
        )

    def coarse(img):
        for copy, _, receives, _ in hand_on(img):
            @pl.when(receives)
            def _(copy=copy):
                copy.wait_recv()

        @pl.when(first)
        def _():
            entry[img] = wide0[img, deep0 - near : deep0 + height + near]

        end = near + height
        for low, high in chunks(0, end + near):
            value = entry[img, low:high].astype(F32)
            state0[low:high] = value
            patch0[0, low:high] = entry[img, low:high]
        for low, high, product in convolved(0, patch0.at[0], 1, end + 1):
            change = (M * STEP) * jnp.tanh(product)
            new = (state0[low:high] + change) + defect0[img, low - 1 : high - 1]
            new = masked(new, low, near, end, above, below)
            state0[low:high] = new
            patch0[1, low:high] = new.astype(BF16)
            a, b = max(low, near), min(high, end)
            out[0, img, a - near : b - near] = new[a - low : b - low]
        ready = list(hand_on(img))
        for low, high, product in list(convolved(M, patch0.at[1], near, end)):
            change = (M * STEP) * jnp.tanh(product)
            rows = slice(low - near, high - near)
            new = (state0[low:high] + change) + defect1[img, rows]
            out[1, img, rows] = new
            leave[img, rows] = new.astype(BF16)
            while ready and ready[0][3] <= high - near:
                copy, sends, _, _ = ready.pop(0)

                @pl.when(sends)
                def _(copy=copy):
                    copy.start()

    def tick(t, carry):
        relaxes = jnp.where(first, t % 2 == 0, t < batch)
        img = jnp.where(first, t // 2, t % batch)

        @pl.when(relaxes)
        def _():
            relax(img)

        @pl.when(jnp.logical_not(relaxes))
        def _():
            coarse(img)

        return carry

    lax.fori_loop(0, 2 * batch, tick, 0)

    for img in range(batch):
        for copy, sends, _ in plan:
            @pl.when(sends)
            def _(img=img, copy=copy):
                copy(img).wait_send()
        for copy, sends, _, _ in hand_on(img):
            @pl.when(sends)
            def _(copy=copy):
                copy.wait_send()


def per_device(sections, bands, weights, image, guess):
    levels, batch, channels, height, breadth = guess.shape
    window = (GROUP + 2) * channels
    narrow = weights.reshape(weights.shape[0], channels, 3, 3, channels)
    narrow = jnp.transpose(narrow, (0, 3, 1, 2, 4)).reshape(weights.shape[0], 3, channels, 3 * channels)
    narrow = jnp.pad(narrow, ((0, 0), (0, 0), (0, 0), (0, window - 3 * channels)))
    moved = jnp.transpose(guess, (0, 1, 3, 2, 4)).astype(BF16)
    picture = jnp.transpose(image, (0, 2, 1, 3)).astype(BF16)
    rows0, rows1 = height + 2 * (M + 1), height + 2 * M
    plane = (channels, breadth)
    result = pl.pallas_call(
        functools.partial(cycle_kernel, sections, bands),
        out_shape=jax.ShapeDtypeStruct((levels, batch, height) + plane, F32),
        in_specs=[pl.BlockSpec(memory_space=pltpu.VMEM)] * 3,
        out_specs=pl.BlockSpec(memory_space=pltpu.VMEM),
        scratch_shapes=[
            pltpu.VMEM((weights.shape[0], 3, GROUP * channels, window), BF16),
            pltpu.VMEM((batch, rows0) + plane, BF16),
            pltpu.VMEM((batch, rows1) + plane, BF16),
            pltpu.VMEM((batch, height + 2 * LEVELS) + plane, BF16),
            pltpu.VMEM((batch, height) + plane, BF16),
            pltpu.VMEM((rows0,) + plane, F32),
            pltpu.VMEM((rows1,) + plane, F32),
            pltpu.VMEM((2, rows0) + plane, BF16),
            pltpu.VMEM((2, rows1) + plane, BF16),
            pltpu.VMEM((batch, height + 2) + plane, F32),
            pltpu.VMEM((batch, height) + plane, F32),
            pltpu.SemaphoreType.DMA((7, batch)),
            pltpu.SemaphoreType.DMA((7, batch)),
            pltpu.SemaphoreType.DMA((4, batch)),
            pltpu.SemaphoreType.DMA((4, batch)),
        ],
        compiler_params=pltpu.CompilerParams(
            collective_id=0, has_side_effects=True, vmem_limit_bytes=40 * 1024 * 1024
        ),
        cost_estimate=pl.CostEstimate(
            flops=2_000_000_000, bytes_accessed=8_000_000, transcendentals=2_500_000
        ),
    )(narrow, moved, picture)
    return jnp.transpose(result, (0, 1, 3, 2, 4))


def solution(mesh):
    sizes = dict(mesh.shape)
    return jax.shard_map(
        functools.partial(per_device, sizes["layer"], sizes["rows"]),
        mesh=mesh,
        in_specs=(
            P("layer", None, None),
            P(None, None, "rows", None),
            P("layer", None, None, "rows", None),
        ),
        out_specs=P("layer", None, None, "rows", None),
        check_vma=False,
    )
```

```python
import functools

import jax
import jax.numpy as jnp
from jax import lax
from jax.experimental import pallas as pl
from jax.experimental.pallas import tpu as pltpu
from jax.sharding import PartitionSpec as P

M = 4
LEVELS = 2
STEP = 0.125
GROUP = 6
MESH = pl.DeviceIdType.MESH
F32 = jnp.float32
BF16 = jnp.bfloat16


def pairs(low, high):
    count = high - low
    upper = -(-count // 4)
    lower = count // 2 - upper
    middle = low + 2 * upper
    return [(low, upper, low - 1, 0), (middle, lower, middle - 1 - (GROUP - lower), GROUP - lower)]


def chunks(low, high):
    return [(start, min(start + GROUP, high)) for start in range(low, high, GROUP)]


def put(patches, start, value):
    count, channels, breadth = value.shape
    flat = value.reshape(count * channels, breadth)
    column = lax.broadcasted_iota(jnp.int32, flat.shape, 1)
    left = jnp.where(column == 0, 0.0, pltpu.roll(flat, 1, 1))
    right = jnp.where(column == breadth - 1, 0.0, pltpu.roll(flat, breadth - 1, 1))
    rows = pl.ds(start, count)
    for place, part in enumerate((left, flat, right)):
        patches[rows, place * channels : (place + 1) * channels, :] = part.reshape(value.shape).astype(BF16)


def conv(matrix_ref, layer, patches, size, window, skip):
    depth, width, breadth = patches.shape
    channels = width // 3
    parts = [
        patches[window + k * size : window + k * size + GROUP + 2].reshape((GROUP + 2) * width, breadth)
        for k in range(2)
    ]
    rows = matrix_ref[layer, skip * channels : (skip + size) * channels, :]
    product = jnp.dot(rows, jnp.concatenate(parts, axis=1), preferred_element_type=F32)
    return [
        product[:, k * breadth : (k + 1) * breadth].reshape(size, channels, breadth) for k in range(2)
    ]


def masked(value, low, first, last, above, below):
    high = low + value.shape[0]
    parts = []
    if low < first:
        parts.append(value[: min(first, high) - low] * above)
    if max(low, first) < min(high, last):
        parts.append(value[max(low, first) - low : min(high, last) - low])
    if high > last:
        parts.append(value[max(low, last) - low :] * below)
    return parts[0] if len(parts) == 1 else jnp.concatenate(parts, axis=0)


def cycle_kernel(
    sections, bands, narrow, guess, image, out,
    matrix, wide0, wide1, entry, leave, state0, state1, patch0, patch1, defect0, defect1,
    start_send, start_recv, chain_send, chain_recv,
):
    batch, height = image.shape[0], image.shape[1]
    s = lax.axis_index("layer")
    r = lax.axis_index("rows")
    above = jnp.where(r > 0, 1.0, 0.0).astype(F32)
    below = jnp.where(r < bands - 1, 1.0, 0.0).astype(F32)
    deep0, deep1, near = M + 1, M, LEVELS

    has = {
        (i, j): functools.reduce(
            jnp.logical_and,
            [c for c in (
                s > 0 if i < 0 else (s < sections - 1 if i > 0 else None),
                r > 0 if j < 0 else (r < bands - 1 if j > 0 else None),
            ) if c is not None],
        )
        for i in (-1, 0, 1) for j in (-1, 0, 1) if (i, j) != (0, 0)
    }

    barrier = pltpu.get_barrier_semaphore()
    total = 0
    for (i, j), there in has.items():
        @pl.when(there)
        def _(i=i, j=j):
            pl.semaphore_signal(barrier, inc=1, device_id=(s + i, r + j), device_id_type=MESH)
        total = total + there.astype(jnp.int32)
    pl.semaphore_wait(barrier, total)

    def start_copy(source, target, slot, img, i, j):
        return pltpu.make_async_remote_copy(
            src_ref=source, dst_ref=target,
            send_sem=start_send.at[slot, img], recv_sem=start_recv.at[slot, img],
            device_id=(s + i, r + j), device_id_type=MESH,
        )

    def band0(img):
        return start_copy(guess.at[1, img], wide0.at[img, pl.ds(deep0, height)], 0, img, 1, 0)

    def down0(img, own):
        source = image.at[img] if own else guess.at[1, img]
        return start_copy(
            source.at[pl.ds(height - deep0, deep0)], wide0.at[img, pl.ds(0, deep0)],
            5 if own else 1, img, 0 if own else 1, 1)

    def up0(img, own):
        source = image.at[img] if own else guess.at[1, img]
        return start_copy(
            source.at[pl.ds(0, deep0)], wide0.at[img, pl.ds(deep0 + height, deep0)],
            6 if own else 2, img, 0 if own else 1, -1)

    def down1(img):
        return start_copy(
            guess.at[0, img, pl.ds(height - deep1, deep1)], wide1.at[img, pl.ds(0, deep1)], 3, img, 0, 1)

    def up1(img):
        return start_copy(
            guess.at[0, img, pl.ds(0, deep1)], wide1.at[img, pl.ds(deep1 + height, deep1)], 4, img, 0, -1)

    first = s == 0
    plan = [
        (band0, s < sections - 1, s > 0),
        (functools.partial(down0, own=True), first & (r < bands - 1), first & (r > 0)),
        (functools.partial(up0, own=True), first & (r > 0), first & (r < bands - 1)),
        (functools.partial(down0, own=False), has[1, 1], has[-1, -1]),
        (functools.partial(up0, own=False), has[1, -1], has[-1, 1]),
        (down1, r < bands - 1, r > 0),
        (up1, r > 0, r < bands - 1),
    ]
    urgent, band, slanted = plan[1:3] + plan[5:], plan[:1], plan[3:5]

    def send(chosen, unless=None):
        for img in range(batch):
            for copy, sends, _ in chosen:
                @pl.when(sends if unless is None else sends & unless)
                def _(img=img, copy=copy):
                    copy(img).start()

    send(urgent)
    send(band)
    send(slanted, jnp.logical_not(first))

    @pl.when(r == 0)
    def _():
        for img in range(batch):
            wide0[img, :deep0] = jnp.zeros((deep0,) + wide0.shape[2:], BF16)
            wide1[img, :deep1] = jnp.zeros((deep1,) + wide1.shape[2:], BF16)
            entry[img, :near] = jnp.zeros((near,) + entry.shape[2:], BF16)

    @pl.when(r == bands - 1)
    def _():
        for img in range(batch):
            wide0[img, deep0 + height :] = jnp.zeros((deep0,) + wide0.shape[2:], BF16)
            wide1[img, deep1 + height :] = jnp.zeros((deep1,) + wide1.shape[2:], BF16)
            entry[img, near + height :] = jnp.zeros((near,) + entry.shape[2:], BF16)

    for img in range(batch):
        wide1[img, deep1 : deep1 + height] = guess[0, img]

    @pl.when(first)
    def _():
        for img in range(batch):
            wide0[img, deep0 : deep0 + height] = image[img]

    channels = narrow.shape[1]
    for layer in range(narrow.shape[0]):
        taps = narrow[layer].astype(F32)
        for k in range(GROUP):
            moved = taps if k == 0 else pltpu.roll(taps, k * 3 * channels, 1)
            matrix[layer, k * channels : (k + 1) * channels, :] = moved.astype(BF16)

    def convolved(layer, patches, low, high):
        for first_row, size, window, skip in pairs(low, high):
            for k, product in enumerate(conv(matrix, layer, patches, size, window, skip)):
                yield first_row + k * size, first_row + (k + 1) * size, product

    def relax(img):
        for copy, _, receives in plan:
            @pl.when(receives)
            def _(copy=copy):
                copy(img).wait_recv()
        anchors = (
            (1, wide1, deep1, state1, patch1, defect1, 0),
            (0, wide0, deep0, state0, patch0, defect0, 1),
        )
        for _, wide, deep, state, patch, _, _ in anchors:
            for low, high in chunks(0, height + 2 * deep):
                value = wide[img, low:high].astype(F32)
                state[low:high] = value
                put(patch.at[0], low, value)
        for j in range(M):
            for point, _, deep, state, patch, defect, extra in anchors:
                end = deep + height
                for low, high, product in convolved(point * M + j, patch.at[j % 2], j + 1, end + deep - j - 1):
                    change = STEP * jnp.tanh(product)
                    old = state[low:high]
                    new = old + change
                    a, b = max(low, deep - extra), min(high, end + extra)
                    if a < b:
                        rows = pl.ds(a - deep + extra, b - a)
                        part = slice(a - low, b - low)
                        if j == 0:
                            defect[img, rows] = -(old + M * change)[part]
                        if j == M - 1:
                            defect[img, rows] = defect[img, rows] + new[part]
                    if j < M - 1:
                        new = masked(new, low, deep, end, above, below)
                        state[low:high] = new
                        put(patch.at[(j + 1) % 2], low, new)

    def chain_copy(source, target, slot, img, j):
        return pltpu.make_async_remote_copy(
            src_ref=leave.at[img, source], dst_ref=entry.at[img, target],
            send_sem=chain_send.at[slot, img], recv_sem=chain_recv.at[slot, img],
            device_id=(s + 1, r + j), device_id_type=MESH,
        )

    def hand_on(img):
        half = height // 2
        return (
            (chain_copy(pl.ds(0, near), pl.ds(near + height, near), 0, img, -1), has[1, -1], has[-1, 1], near),
            (chain_copy(pl.ds(0, half), pl.ds(near, half), 1, img, 0), has[1, 0], has[-1, 0], half),
            (chain_copy(pl.ds(height - near, near), pl.ds(0, near), 2, img, 1), has[1, 1], has[-1, -1], height),
            (chain_copy(pl.ds(half, height - half), pl.ds(near + half, height - half), 3, img, 0),
             has[1, 0], has[-1, 0], height),
        )

    def coarse(img):
        for copy, _, receives, _ in hand_on(img):
            @pl.when(receives)
            def _(copy=copy):
                copy.wait_recv()

        @pl.when(first)
        def _():
            entry[img] = wide0[img, deep0 - near : deep0 + height + near]

        end = near + height
        for low, high in chunks(0, end + near):
            value = entry[img, low:high].astype(F32)
            state0[low:high] = value
            put(patch0.at[0], low, value)
        for low, high, product in convolved(0, patch0.at[0], 1, end + 1):
            change = (M * STEP) * jnp.tanh(product)
            new = (state0[low:high] + change) + defect0[img, low - 1 : high - 1]
            new = masked(new, low, near, end, above, below)
            state0[low:high] = new
            put(patch0.at[1], low, new)
            a, b = max(low, near), min(high, end)
            out[0, img, a - near : b - near] = new[a - low : b - low]
        ready = list(hand_on(img))
        for low, high, product in convolved(M, patch0.at[1], near, end):
            change = (M * STEP) * jnp.tanh(product)
            rows = slice(low - near, high - near)
            new = (state0[low:high] + change) + defect1[img, rows]
            out[1, img, rows] = new
            leave[img, rows] = new.astype(BF16)
            while ready and ready[0][3] <= high - near:
                copy, sends, _, _ = ready.pop(0)

                @pl.when(sends)
                def _(copy=copy):
                    copy.start()

    def tick(t, carry):
        relaxes = jnp.where(first, t % 2 == 0, t < batch)
        img = jnp.where(first, t // 2, t % batch)

        @pl.when(relaxes)
        def _():
            relax(img)

        @pl.when(jnp.logical_not(relaxes))
        def _():
            coarse(img)

        @pl.when(first & (t == 0))
        def _():
            send(slanted)

        return carry

    lax.fori_loop(0, 2 * batch, tick, 0)

    for img in range(batch):
        for copy, sends, _ in plan:
            @pl.when(sends)
            def _(img=img, copy=copy):
                copy(img).wait_send()
        for copy, sends, _, _ in hand_on(img):
            @pl.when(sends)
            def _(copy=copy):
                copy.wait_send()


def per_device(sections, bands, weights, image, guess):
    levels, batch, channels, height, breadth = guess.shape
    window = (GROUP + 2) * 3 * channels
    narrow = jnp.pad(weights, ((0, 0), (0, 0), (0, window - weights.shape[2])))
    moved = jnp.transpose(guess, (0, 1, 3, 2, 4)).astype(BF16)
    picture = jnp.transpose(image, (0, 2, 1, 3)).astype(BF16)
    rows0, rows1 = height + 2 * (M + 1), height + 2 * M
    plane = (channels, breadth)
    wide_plane = (3 * channels, breadth)
    result = pl.pallas_call(
        functools.partial(cycle_kernel, sections, bands),
        out_shape=jax.ShapeDtypeStruct((levels, batch, height) + plane, F32),
        in_specs=[pl.BlockSpec(memory_space=pltpu.VMEM)] * 3,
        out_specs=pl.BlockSpec(memory_space=pltpu.VMEM),
        scratch_shapes=[
            pltpu.VMEM((weights.shape[0], GROUP * channels, window), BF16),
            pltpu.VMEM((batch, rows0) + plane, BF16),
            pltpu.VMEM((batch, rows1) + plane, BF16),
            pltpu.VMEM((batch, height + 2 * LEVELS) + plane, BF16),
            pltpu.VMEM((batch, height) + plane, BF16),
            pltpu.VMEM((rows0,) + plane, F32),
            pltpu.VMEM((rows1,) + plane, F32),
            pltpu.VMEM((2, rows0) + wide_plane, BF16),
            pltpu.VMEM((2, rows1) + wide_plane, BF16),
            pltpu.VMEM((batch, height + 2) + plane, F32),
            pltpu.VMEM((batch, height) + plane, F32),
            pltpu.SemaphoreType.DMA((7, batch)),
            pltpu.SemaphoreType.DMA((7, batch)),
            pltpu.SemaphoreType.DMA((4, batch)),
            pltpu.SemaphoreType.DMA((4, batch)),
        ],
        compiler_params=pltpu.CompilerParams(
            collective_id=0, has_side_effects=True, vmem_limit_bytes=40 * 1024 * 1024
        ),
        cost_estimate=pl.CostEstimate(
            flops=2_000_000_000, bytes_accessed=8_000_000, transcendentals=2_500_000
        ),
    )(narrow, moved, picture)
    return jnp.transpose(result, (0, 1, 3, 2, 4))


def solution(mesh):
    sizes = dict(mesh.shape)
    return jax.shard_map(
        functools.partial(per_device, sizes["layer"], sizes["rows"]),
        mesh=mesh,
        in_specs=(
            P("layer", None, None),
            P(None, None, "rows", None),
            P("layer", None, None, "rows", None),
        ),
        out_specs=P("layer", None, None, "rows", None),
        check_vma=False,
    )
```

```python
import functools

import jax
import jax.numpy as jnp
from jax import lax
from jax.experimental import pallas as pl
from jax.experimental.pallas import tpu as pltpu
from jax.sharding import PartitionSpec as P

M = 4
LEVELS = 2
STEP = 0.125
GROUP = 6
MESH = pl.DeviceIdType.MESH
F32 = jnp.float32
BF16 = jnp.bfloat16


def pairs(low, high):
    count = high - low
    upper = -(-count // 4)
    lower = count // 2 - upper
    middle = low + 2 * upper
    return [(low, upper, low - 1, 0), (middle, lower, middle - 1 - (GROUP - lower), GROUP - lower)]


def chunks(low, high):
    return [(start, min(start + GROUP, high)) for start in range(low, high, GROUP)]


def put(patches, start, value):
    count, channels, breadth = value.shape
    flat = value.reshape(count * channels, breadth)
    column = lax.broadcasted_iota(jnp.int32, flat.shape, 1)
    left = jnp.where(column == 0, 0.0, pltpu.roll(flat, 1, 1))
    right = jnp.where(column == breadth - 1, 0.0, pltpu.roll(flat, breadth - 1, 1))
    rows = pl.ds(start, count)
    for place, part in enumerate((left, flat, right)):
        patches[rows, place * channels : (place + 1) * channels, :] = part.reshape(value.shape).astype(BF16)


def conv(matrix_ref, layer, patches, size, window, skip):
    depth, width, breadth = patches.shape
    channels = width // 3
    parts = [
        patches[window + k * size : window + k * size + GROUP + 2].reshape((GROUP + 2) * width, breadth)
        for k in range(2)
    ]
    rows = matrix_ref[layer, skip * channels : (skip + size) * channels, :]
    product = jnp.dot(rows, jnp.concatenate(parts, axis=1), preferred_element_type=F32)
    return [
        product[:, k * breadth : (k + 1) * breadth].reshape(size, channels, breadth) for k in range(2)
    ]


def masked(value, low, first, last, above, below):
    high = low + value.shape[0]
    parts = []
    if low < first:
        parts.append(value[: min(first, high) - low] * above)
    if max(low, first) < min(high, last):
        parts.append(value[max(low, first) - low : min(high, last) - low])
    if high > last:
        parts.append(value[max(low, last) - low :] * below)
    return parts[0] if len(parts) == 1 else jnp.concatenate(parts, axis=0)


def cycle_kernel(
    sections, bands, narrow, guess, image, out,
    matrix, wide0, wide1, entry, leave, state0, state1, patch0, patch1, defect0, defect1,
    start_send, start_recv, chain_send, chain_recv,
):
    batch, height = image.shape[0], image.shape[1]
    s = lax.axis_index("layer")
    r = lax.axis_index("rows")
    above = jnp.where(r > 0, 1.0, 0.0).astype(F32)
    below = jnp.where(r < bands - 1, 1.0, 0.0).astype(F32)
    deep0, deep1, near = M + 1, M, LEVELS

    has = {
        (i, j): functools.reduce(
            jnp.logical_and,
            [c for c in (
                s > 0 if i < 0 else (s < sections - 1 if i > 0 else None),
                r > 0 if j < 0 else (r < bands - 1 if j > 0 else None),
            ) if c is not None],
        )
        for i in (-1, 0, 1) for j in (-1, 0, 1) if (i, j) != (0, 0)
    }

    barrier = pltpu.get_barrier_semaphore()
    total = 0
    for (i, j), there in has.items():
        @pl.when(there)
        def _(i=i, j=j):
            pl.semaphore_signal(barrier, inc=1, device_id=(s + i, r + j), device_id_type=MESH)
        total = total + there.astype(jnp.int32)
    pl.semaphore_wait(barrier, total)

    def start_copy(source, target, slot, img, i, j):
        return pltpu.make_async_remote_copy(
            src_ref=source, dst_ref=target,
            send_sem=start_send.at[slot, img], recv_sem=start_recv.at[slot, img],
            device_id=(s + i, r + j), device_id_type=MESH,
        )

    def band0(img):
        return start_copy(guess.at[1, img], wide0.at[img, pl.ds(deep0, height)], 0, img, 1, 0)

    def down0(img, own):
        source = image.at[img] if own else guess.at[1, img]
        return start_copy(
            source.at[pl.ds(height - deep0, deep0)], wide0.at[img, pl.ds(0, deep0)],
            5 if own else 1, img, 0 if own else 1, 1)

    def up0(img, own):
        source = image.at[img] if own else guess.at[1, img]
        return start_copy(
            source.at[pl.ds(0, deep0)], wide0.at[img, pl.ds(deep0 + height, deep0)],
            6 if own else 2, img, 0 if own else 1, -1)

    def down1(img):
        return start_copy(
            guess.at[0, img, pl.ds(height - deep1, deep1)], wide1.at[img, pl.ds(0, deep1)], 3, img, 0, 1)

    def up1(img):
        return start_copy(
            guess.at[0, img, pl.ds(0, deep1)], wide1.at[img, pl.ds(deep1 + height, deep1)], 4, img, 0, -1)

    first = s == 0
    plan = [
        (band0, s < sections - 1, s > 0),
        (functools.partial(down0, own=True), first & (r < bands - 1), first & (r > 0)),
        (functools.partial(up0, own=True), first & (r > 0), first & (r < bands - 1)),
        (functools.partial(down0, own=False), has[1, 1], has[-1, -1]),
        (functools.partial(up0, own=False), has[1, -1], has[-1, 1]),
        (down1, r < bands - 1, r > 0),
        (up1, r > 0, r < bands - 1),
    ]
    for img in range(batch):
        for copy, sends, _ in plan:
            @pl.when(sends)
            def _(img=img, copy=copy):
                copy(img).start()

    @pl.when(r == 0)
    def _():
        for img in range(batch):
            wide0[img, :deep0] = jnp.zeros((deep0,) + wide0.shape[2:], BF16)
            wide1[img, :deep1] = jnp.zeros((deep1,) + wide1.shape[2:], BF16)
            entry[img, :near] = jnp.zeros((near,) + entry.shape[2:], BF16)

    @pl.when(r == bands - 1)
    def _():
        for img in range(batch):
            wide0[img, deep0 + height :] = jnp.zeros((deep0,) + wide0.shape[2:], BF16)
            wide1[img, deep1 + height :] = jnp.zeros((deep1,) + wide1.shape[2:], BF16)
            entry[img, near + height :] = jnp.zeros((near,) + entry.shape[2:], BF16)

    for img in range(batch):
        wide1[img, deep1 : deep1 + height] = guess[0, img]

    @pl.when(first)
    def _():
        for img in range(batch):
            wide0[img, deep0 : deep0 + height] = image[img]

    channels, reach = narrow.shape[1:]
    whole = matrix.shape[2]
    tile = 128
    for layer in range(narrow.shape[0]):
        taps = narrow[layer].astype(F32)
        for k in range(GROUP):
            whole_tiles, rest = divmod(k * 3 * channels, tile)
            origin = whole_tiles * tile
            moved = (pltpu.roll(taps, rest, 1) if rest else taps).astype(BF16)
            parts = [jnp.zeros((channels, origin), BF16)] if origin else []
            parts.append(moved)
            if origin + reach < whole:
                parts.append(jnp.zeros((channels, whole - origin - reach), BF16))
            matrix[layer, k * channels : (k + 1) * channels, :] = jnp.concatenate(parts, axis=1)

    def convolved(layer, patches, low, high):
        for first_row, size, window, skip in pairs(low, high):
            for k, product in enumerate(conv(matrix, layer, patches, size, window, skip)):
                yield first_row + k * size, first_row + (k + 1) * size, product

    def relax(img):
        for copy, _, receives in plan:
            @pl.when(receives)
            def _(copy=copy):
                copy(img).wait_recv()
        anchors = (
            (1, wide1, deep1, state1, patch1, defect1, 0),
            (0, wide0, deep0, state0, patch0, defect0, 1),
        )
        for _, wide, deep, state, patch, _, _ in anchors:
            for low, high in chunks(0, height + 2 * deep):
                value = wide[img, low:high].astype(F32)
                state[low:high] = value
                put(patch.at[0], low, value)
        for j in range(M):
            for point, _, deep, state, patch, defect, extra in anchors:
                end = deep + height
                for low, high, product in convolved(point * M + j, patch.at[j % 2], j + 1, end + deep - j - 1):
                    change = STEP * jnp.tanh(product)
                    old = state[low:high]
                    new = old + change
                    a, b = max(low, deep - extra), min(high, end + extra)
                    if a < b:
                        rows = pl.ds(a - deep + extra, b - a)
                        part = slice(a - low, b - low)
                        if j == 0:
                            defect[img, rows] = -(old + M * change)[part]
                        if j == M - 1:
                            defect[img, rows] = defect[img, rows] + new[part]
                    if j < M - 1:
                        new = masked(new, low, deep, end, above, below)
                        state[low:high] = new
                        put(patch.at[(j + 1) % 2], low, new)

    def chain_copy(source, target, slot, img, j):
        return pltpu.make_async_remote_copy(
            src_ref=leave.at[img, source], dst_ref=entry.at[img, target],
            send_sem=chain_send.at[slot, img], recv_sem=chain_recv.at[slot, img],
            device_id=(s + 1, r + j), device_id_type=MESH,
        )

    def hand_on(img):
        half = height // 2
        return (
            (chain_copy(pl.ds(0, near), pl.ds(near + height, near), 0, img, -1), has[1, -1], has[-1, 1], near),
            (chain_copy(pl.ds(0, half), pl.ds(near, half), 1, img, 0), has[1, 0], has[-1, 0], half),
            (chain_copy(pl.ds(height - near, near), pl.ds(0, near), 2, img, 1), has[1, 1], has[-1, -1], height),
            (chain_copy(pl.ds(half, height - half), pl.ds(near + half, height - half), 3, img, 0),
             has[1, 0], has[-1, 0], height),
        )

    def coarse(img):
        for copy, _, receives, _ in hand_on(img):
            @pl.when(receives)
            def _(copy=copy):
                copy.wait_recv()

        @pl.when(first)
        def _():
            entry[img] = wide0[img, deep0 - near : deep0 + height + near]

        end = near + height
        for low, high in chunks(0, end + near):
            value = entry[img, low:high].astype(F32)
            state0[low:high] = value
            put(patch0.at[0], low, value)
        for low, high, product in convolved(0, patch0.at[0], 1, end + 1):
            change = (M * STEP) * jnp.tanh(product)
            new = (state0[low:high] + change) + defect0[img, low - 1 : high - 1]
            new = masked(new, low, near, end, above, below)
            state0[low:high] = new
            put(patch0.at[1], low, new)
            a, b = max(low, near), min(high, end)
            out[0, img, a - near : b - near] = new[a - low : b - low]
        ready = list(hand_on(img))
        for low, high, product in convolved(M, patch0.at[1], near, end):
            change = (M * STEP) * jnp.tanh(product)
            rows = slice(low - near, high - near)
            new = (state0[low:high] + change) + defect1[img, rows]
            out[1, img, rows] = new
            leave[img, rows] = new.astype(BF16)
            while ready and ready[0][3] <= high - near:
                copy, sends, _, _ = ready.pop(0)

                @pl.when(sends)
                def _(copy=copy):
                    copy.start()

    def tick(t, carry):
        relaxes = jnp.where(first, t % 2 == 0, t < batch)
        img = jnp.where(first, t // 2, t % batch)

        @pl.when(relaxes)
        def _():
            relax(img)

        @pl.when(jnp.logical_not(relaxes))
        def _():
            coarse(img)

        return carry

    lax.fori_loop(0, 2 * batch, tick, 0)

    for img in range(batch):
        for copy, sends, _ in plan:
            @pl.when(sends)
            def _(img=img, copy=copy):
                copy(img).wait_send()
        for copy, sends, _, _ in hand_on(img):
            @pl.when(sends)
            def _(copy=copy):
                copy.wait_send()


def per_device(sections, bands, weights, image, guess):
    levels, batch, channels, height, breadth = guess.shape
    window = (GROUP + 2) * 3 * channels
    narrow = jnp.pad(weights, ((0, 0), (0, 0), (0, 3 * channels)))
    moved = jnp.transpose(guess, (0, 1, 3, 2, 4)).astype(BF16)
    picture = jnp.transpose(image, (0, 2, 1, 3)).astype(BF16)
    rows0, rows1 = height + 2 * (M + 1), height + 2 * M
    plane = (channels, breadth)
    wide_plane = (3 * channels, breadth)
    result = pl.pallas_call(
        functools.partial(cycle_kernel, sections, bands),
        out_shape=jax.ShapeDtypeStruct((levels, batch, height) + plane, F32),
        in_specs=[pl.BlockSpec(memory_space=pltpu.VMEM)] * 3,
        out_specs=pl.BlockSpec(memory_space=pltpu.VMEM),
        scratch_shapes=[
            pltpu.VMEM((weights.shape[0], GROUP * channels, window), BF16),
            pltpu.VMEM((batch, rows0) + plane, BF16),
            pltpu.VMEM((batch, rows1) + plane, BF16),
            pltpu.VMEM((batch, height + 2 * LEVELS) + plane, BF16),
            pltpu.VMEM((batch, height) + plane, BF16),
            pltpu.VMEM((rows0,) + plane, F32),
            pltpu.VMEM((rows1,) + plane, F32),
            pltpu.VMEM((2, rows0) + wide_plane, BF16),
            pltpu.VMEM((2, rows1) + wide_plane, BF16),
            pltpu.VMEM((batch, height + 2) + plane, F32),
            pltpu.VMEM((batch, height) + plane, F32),
            pltpu.SemaphoreType.DMA((7, batch)),
            pltpu.SemaphoreType.DMA((7, batch)),
            pltpu.SemaphoreType.DMA((4, batch)),
            pltpu.SemaphoreType.DMA((4, batch)),
        ],
        compiler_params=pltpu.CompilerParams(
            collective_id=0, has_side_effects=True, vmem_limit_bytes=40 * 1024 * 1024
        ),
        cost_estimate=pl.CostEstimate(
            flops=2_000_000_000, bytes_accessed=8_000_000, transcendentals=2_500_000
        ),
    )(narrow, moved, picture)
    return jnp.transpose(result, (0, 1, 3, 2, 4))


def solution(mesh):
    sizes = dict(mesh.shape)
    return jax.shard_map(
        functools.partial(per_device, sizes["layer"], sizes["rows"]),
        mesh=mesh,
        in_specs=(
            P("layer", None, None),
            P(None, None, "rows", None),
            P("layer", None, None, "rows", None),
        ),
        out_specs=P("layer", None, None, "rows", None),
        check_vma=False,
    )
```
